32 devices in a mesh: br: 4 (over y, x), bus: 8 (over z, core).
Axes of the slice: x: 2, y: 2, z: 4, core: 2. Of those that a mesh axis runs over, the one named last changes fastest.
Arguments:
- ptdf: bfloat16 [8192, 65536], P('br', 'bus'), may hold values from -0.0234375 to 0.0234375
- load_codes: int32 [65536, 1024], P('bus'), may hold values from -4096 to 4096
- limit_codes: int32 [8192], P('br'), may hold values from 64 to 320
Outputs:
- penalty: float32 [8192, 1024], P(('br', 'bus'))
- sensitivity: float32 [65536, 1024], P('bus', 'br')
The draws below stay inside these ranges and needn't reach their ends.
All inputs are finite; a program needn't handle non-finite values.
Results may differ from the reference program's by a relative error of at most 0.004.
Values may be sent and summed in bfloat16 or wider, within the bound.
No kernel may reach another device: no remote copies, remote signals or barrier semaphores. Data moves between devices by JAX's collectives and lax.ppermute only.
A program may use at most 192 MiB of HBM per device.

```python
import jax
import jax.numpy as jnp
from jax import lax

NB = 65536
BR = 8192
HOURS = 1024


def with_ends(drawn, stream_key, smallest, largest):
    longest = drawn.shape.index(max(drawn.shape))
    spots = []
    for shift in (0, 1):
        where = [jax.random.randint(jax.random.fold_in(stream_key, axis), (), 0, length) for axis, length in enumerate(drawn.shape)]
        where[longest] = (where[longest] + shift) % drawn.shape[longest]
        spots.append(tuple(where))
    return drawn.at[spots[0]].set(smallest).at[spots[1]].set(largest)


def steps_of(key, shape, split, least, high):
    factor_of = 1.0
    for axis_at, parts in split:
        heights = jax.random.uniform(jax.random.fold_in(jax.random.fold_in(key, 6), axis_at), (parts,), jnp.float32, least / len(split), high / len(split))
        factor_of = factor_of * jnp.repeat(jnp.exp(heights), shape[axis_at] // parts).reshape((-1,) + (1,) * (len(shape) - 1 - axis_at))
    return factor_of


def bell_draw(own_key, shape, deviation, limit, cuts=(), kind=jnp.bfloat16):
    array = deviation * jax.random.normal(own_key, shape, jnp.float32)
    if cuts:
        array = array * steps_of(own_key, shape, cuts, -0.22, 0.18)
    return jnp.clip(array, -limit, limit).astype(kind)


def setup_inputs(seed: int = 0) -> dict:
    streams_of = jax.random.split(jax.random.key(seed), 4)
    return {
        "ptdf": bell_draw(streams_of[0], (BR, NB), NB ** -0.5, 0.0234375, ((0, 4), (1, 8))),
        "load_codes": with_ends(jax.random.randint(streams_of[1], (NB, HOURS), -4096, 4097), jax.random.fold_in(streams_of[1], 1), -4096, 4096).astype(jnp.int32),
        "limit_codes": with_ends(jax.random.randint(streams_of[2], (BR,), 64, 321), jax.random.fold_in(streams_of[2], 1), 64, 320).astype(jnp.int32),
    }


def reference(ptdf, load_codes, limit_codes):
    injections = (load_codes.astype(jnp.float32) / 1024.0).astype(jnp.bfloat16)
    flows = jnp.dot(ptdf, injections, preferred_element_type=jnp.float32)
    limits = (limit_codes.astype(jnp.float32) / 64.0)[:, None]
    magnitude = jnp.sqrt(flows * flows + 1.0)
    zvalue = 4.0 * (magnitude / limits - 1.0)
    penalty = jax.nn.softplus(zvalue) / 4.0
    adjoint = (jax.nn.sigmoid(zvalue) * flows / (magnitude * limits)).astype(jnp.bfloat16)
    sensitivity = lax.dot_general(ptdf, adjoint, (((0,), (0,)), ((), ())), preferred_element_type=jnp.float32)
    return (penalty, sensitivity)
```

```python
import functools

import jax
import jax.numpy as jnp
from jax import lax
from jax.experimental import pallas as pl
from jax.experimental.pallas import tpu as pltpu
from jax.sharding import PartitionSpec as P

MIB = 2**20
VMEM = 56 * MIB


def params():
    return pltpu.CompilerParams(vmem_limit_bytes=VMEM)


def cost(flops, nbytes, trans=0):
    return pl.CostEstimate(flops=int(flops), bytes_accessed=int(nbytes), transcendentals=int(trans))


def penalty_and_adjoint(flows, limits):
    magnitude = jnp.sqrt(flows * flows + 1.0)
    zvalue = 4.0 * (magnitude / limits - 1.0)
    penalty = (jnp.maximum(zvalue, 0.0) + jnp.log1p(jnp.exp(-jnp.abs(zvalue)))) * 0.25
    adjoint = (jax.nn.sigmoid(zvalue) * flows / (magnitude * limits)).astype(jnp.bfloat16)
    return penalty, adjoint


def flows_kernel(groups, chips, own, pos, ptdf, *refs):
    codes, (keep, away, total) = refs[:groups], refs[groups:]
    k = pl.program_id(0)
    wide = codes[0].shape[1]
    for g in range(groups):
        injections = (codes[g][...].astype(jnp.float32) * (1.0 / 1024.0)).astype(jnp.bfloat16)
        part = jnp.dot(ptdf[...], injections, preferred_element_type=jnp.float32)
        cols = slice(g * wide, (g + 1) * wide)

        @pl.when(k == 0)
        def _():
            total[:, cols] = part

        @pl.when(k > 0)
        def _():
            total[:, cols] += part

    @pl.when(k == pl.num_programs(0) - 1)
    def _():
        core = pos[1]
        for chip in range(chips):
            rows = slice(chip * own, (chip + 1) * own)
            keep[rows, :] = total[pl.ds(pl.multiple_of((2 * chip + core) * own, own), own), :]
            away[rows, :] = total[pl.ds(pl.multiple_of((2 * chip + 1 - core) * own, own), own), :]


def partial_flows(pos, ptdf, codes, first, groups, wide, chips, depth):
    rows, buses = ptdf.shape
    own = rows // (2 * chips)
    hours = groups * wide
    half = jax.ShapeDtypeStruct((rows // 2, hours), jnp.float32)
    spec = pl.BlockSpec((rows // 2, hours), lambda k, pos: (0, 0))
    return pl.pallas_call(
        functools.partial(flows_kernel, groups, chips, own),
        out_shape=(half, half),
        grid_spec=pltpu.PrefetchScalarGridSpec(
            num_scalar_prefetch=1,
            grid=(buses // depth,),
            in_specs=[pl.BlockSpec((rows, depth), lambda k, pos: (0, k))]
            + [pl.BlockSpec((depth, wide), lambda k, pos, g=g: (k, pos[first + g])) for g in range(groups)],
            out_specs=(spec, spec),
            scratch_shapes=[pltpu.VMEM((rows, hours), jnp.float32)],
        ),
        compiler_params=params(),
        cost_estimate=cost(2 * rows * buses * hours, 2 * rows * buses + 4 * buses * hours),
        name="flows",
    )(pos, ptdf, *[codes] * groups)


def pair_kernel(chips, pos, keep, came, mine, *sends):
    chip, own = pos[0], mine.shape[0]
    for k in range(chips):
        rows = pl.ds(pl.multiple_of(lax.rem(chip + k, chips) * own, own), own)
        both = keep[rows, :] + came[rows, :]
        if k == 0:
            mine[...] = both
        else:
            sends[k - 1][...] = both.astype(jnp.bfloat16)


def pair_sum(pos, keep, came, chips):
    rows, hours = keep.shape
    own = rows // chips
    vmem = pl.BlockSpec(memory_space=pltpu.VMEM)
    return pl.pallas_call(
        functools.partial(pair_kernel, chips),
        out_shape=[jax.ShapeDtypeStruct((own, hours), jnp.float32)]
        + [jax.ShapeDtypeStruct((own, hours), jnp.bfloat16)] * (chips - 1),
        in_specs=[pl.BlockSpec(memory_space=pltpu.SMEM), vmem, vmem],
        out_specs=[vmem] * chips,
        compiler_params=params(),
        cost_estimate=cost(rows * hours, 10 * rows * hours),
        name="pair_sum",
    )(pos, keep, came)


def overload_kernel(others, pos, limits, mine, *refs):
    came, (penalty, adjoint) = refs[:others], refs[-2:]
    flows = mine[...]
    for part in came:
        flows += part[...].astype(jnp.float32)
    penalty[...], adjoint[...] = penalty_and_adjoint(flows, limits[...])


def overload(pos, limits, mine, came, penalty, hours_all, first, groups, wide):
    own = mine.shape[0]
    block = pl.BlockSpec((own, wide), lambda g, pos: (0, g))
    place = pl.BlockSpec((own, wide), lambda g, pos: (0, pos[first + g]))
    operands = [pos, limits, mine, *came]
    in_specs = [pl.BlockSpec((own, 1), lambda g, pos: (0, 0))] + [block] * (1 + len(came))
    aliases = {}
    if penalty is not None:
        aliases = {len(operands): 0}
        operands.append(penalty)
        in_specs.append(pl.BlockSpec(memory_space=pl.ANY))
    return pl.pallas_call(
        functools.partial(overload_kernel, len(came)),
        out_shape=(
            jax.ShapeDtypeStruct((own, hours_all), jnp.float32),
            jax.ShapeDtypeStruct(mine.shape, jnp.bfloat16),
        ),
        grid_spec=pltpu.PrefetchScalarGridSpec(
            num_scalar_prefetch=1, grid=(groups,), in_specs=in_specs, out_specs=(place, block)
        ),
        input_output_aliases=aliases,
        compiler_params=params(),
        cost_estimate=cost(20 * mine.size, 16 * mine.size, 4 * mine.size),
        name="overload",
    )(*operands)


def sens_kernel(chips, own, adds, final, pos, ptdf, *refs):
    mine, swapped = refs[:chips], refs[chips : 2 * chips]
    extra, (out, adjoint) = refs[2 * chips : 2 * chips + adds], refs[-2:]

    @pl.when(pl.program_id(0) == 0)
    def _():
        chip, core = pos[0], pos[1]
        for k in range(chips):
            slot = 2 * lax.rem(chip + chips - k, chips)
            adjoint[pl.ds(pl.multiple_of((slot + core) * own, own), own), :] = mine[k][...]
            adjoint[pl.ds(pl.multiple_of((slot + 1 - core) * own, own), own), :] = swapped[k][...]

    part = lax.dot_general(
        ptdf[...], adjoint[...], (((0,), (0,)), ((), ())), preferred_element_type=jnp.float32
    )
    for other in extra:
        part += other[...].astype(jnp.float32)
    out[...] = part.astype(out.dtype)


def partial_sens(pos, ptdf, mine, swapped, column, wide, half, block, adds=(), into=None, final=False):
    chips = len(mine)
    rows, buses = ptdf.shape
    own = rows // (2 * chips)
    steps = buses // 2 // block
    place = pl.BlockSpec((block, wide), lambda i, pos: (half * steps + i, 0))
    local = pl.BlockSpec((block, wide), lambda i, pos: (i, 0))
    operands = [pos, ptdf, *mine, *swapped, *adds]
    in_specs = (
        [pl.BlockSpec((rows, block), lambda i, pos: (0, half * steps + i))]
        + [pl.BlockSpec((own, wide), lambda i, pos: (0, column))] * (2 * chips)
        + [local] * len(adds)
    )
    aliases = {}
    if into is not None:
        aliases = {len(operands): 0}
        operands.append(into)
        in_specs.append(pl.BlockSpec(memory_space=pl.ANY))
    return pl.pallas_call(
        functools.partial(sens_kernel, chips, own, len(adds), final),
        out_shape=jax.ShapeDtypeStruct((buses, wide), jnp.float32)
        if final
        else jax.ShapeDtypeStruct((buses // 2, wide), jnp.bfloat16),
        grid_spec=pltpu.PrefetchScalarGridSpec(
            num_scalar_prefetch=1,
            grid=(steps,),
            in_specs=in_specs,
            out_specs=place if final else local,
            scratch_shapes=[pltpu.VMEM((rows, wide), jnp.bfloat16)],
        ),
        input_output_aliases=aliases,
        compiler_params=params(),
        cost_estimate=cost(rows * buses * wide, rows * buses + buses * wide),
        name="sens",
    )(*operands)


def add_kernel(total, came, out):
    out[...] = total[...] + came[...].astype(jnp.float32)


def add_into(total, came, half, block):
    rows, wide = came.shape
    steps = rows // block
    place = pl.BlockSpec((block, wide), lambda i: (half * steps + i, 0))
    return pl.pallas_call(
        add_kernel,
        out_shape=jax.ShapeDtypeStruct(total.shape, total.dtype),
        grid=(steps,),
        in_specs=[place, pl.BlockSpec((block, wide), lambda i: (i, 0))],
        out_specs=place,
        input_output_aliases={0: 0},
        compiler_params=params(),
        cost_estimate=cost(came.size, 10 * came.size),
        name="add_last",
    )(total, came)


def local_tree(ptdf, load_codes, limit_codes):
    cores = lax.axis_size("bus")
    chips = cores // 2
    rows, buses = ptdf.shape
    hours_all = load_codes.shape[1]
    own = rows // cores
    wide = hours_all // 4
    me, spot = lax.axis_index("br"), lax.axis_index("bus")
    far, over, up, home = me ^ 3, me ^ 1, me ^ 2, me
    pos = jnp.stack([spot // 2, spot % 2, far, over, up, home]).astype(jnp.int32)
    limits = lax.dynamic_slice_in_dim(limit_codes, spot * own, own, 0).astype(jnp.float32)[:, None] / 64.0
    depth = min(1024, buses)
    block = min(1024, buses // 2)

    def across(x, bit):
        return lax.ppermute(x, "br", [(i, i ^ bit) for i in range(4)])

    def swap(x):
        return lax.ppermute(x, "bus", [(i, i ^ 1) for i in range(cores)])

    def along(x, k):
        return lax.ppermute(x, "bus", [(i, (i + 2 * k) % cores) for i in range(cores)])

    def adjoints(first, groups, penalty):
        keep, away = partial_flows(pos, ptdf, load_codes, first, groups, wide, chips, depth)
        mine, *sends = pair_sum(pos, keep, swap(away), chips)
        came = [along(sends[k - 1], k) for k in range(1, chips)]
        penalty, adjoint = overload(pos, limits, mine, came, penalty, hours_all, first, groups, wide)
        held = [adjoint] + [along(adjoint, k) for k in range(1, chips)]
        return penalty, (held, [swap(x) for x in held])

    def sens(adjoint, column, half, **more):
        return partial_sens(pos, ptdf, *adjoint, column, wide, half, block, **more)

    penalty, adj_far = adjoints(2, 1, None)
    far_a = across(sens(adj_far, 0, 0), 1)
    far_b = across(sens(adj_far, 0, 1), 2)
    penalty, adj_mid = adjoints(3, 2, penalty)
    over_a = across(sens(adj_mid, 0, 0), 1)
    up_b = across(sens(adj_mid, 1, 1), 2)
    penalty, adj_home = adjoints(5, 1, penalty)
    up_a = across(sens(adj_mid, 1, 0, adds=(far_a,)), 2)
    over_b = across(sens(adj_mid, 0, 1, adds=(far_b,)), 1)
    total = sens(adj_home, 0, 0, adds=(over_a,), final=True)
    total = sens(adj_home, 0, 1, adds=(up_b,), final=True, into=total)
    total = add_into(total, up_a, 0, block)
    total = add_into(total, over_b, 1, block)
    return penalty, total


def local_general(ptdf, load_codes, limit_codes):
    own = ptdf.shape[0] // lax.axis_size("bus")
    injections = (load_codes.astype(jnp.float32) / 1024.0).astype(jnp.bfloat16)
    partial_flow = jnp.dot(ptdf, injections, preferred_element_type=jnp.float32)
    flows = lax.psum_scatter(partial_flow, "bus", scatter_dimension=0, tiled=True)
    codes = lax.dynamic_slice_in_dim(limit_codes, lax.axis_index("bus") * own, own, 0)
    penalty, mine = penalty_and_adjoint(flows, codes.astype(jnp.float32)[:, None] / 64.0)
    adjoint = lax.all_gather(mine, "bus", axis=0, tiled=True)
    part = lax.dot_general(
        ptdf, adjoint, (((0,), (0,)), ((), ())), preferred_element_type=jnp.float32
    )
    return penalty, lax.psum_scatter(part, "br", scatter_dimension=1, tiled=True)


def solution(mesh):
    tree = mesh.shape["br"] == 4 and mesh.shape["bus"] % 2 == 0
    return jax.shard_map(
        local_tree if tree else local_general,
        mesh=mesh,
        in_specs=(P("br", "bus"), P("bus", None), P("br")),
        out_specs=(P(("br", "bus"), None), P("bus", "br")),
        check_vma=False,
    )
```

```python
import functools

import jax
import jax.numpy as jnp
from jax import lax
from jax.experimental import pallas as pl
from jax.experimental.pallas import tpu as pltpu
from jax.sharding import PartitionSpec as P

MIB = 2**20
HASTE = 0.4
HBM = pl.BlockSpec(memory_space=pl.ANY)
FAST = pl.BlockSpec(memory_space=pltpu.VMEM)
WORDS = pl.BlockSpec(memory_space=pltpu.SMEM)
BF16, F32 = jnp.bfloat16, jnp.float32


def cost(flops, nbytes):
    return pl.CostEstimate(flops=int(flops * HASTE), bytes_accessed=int(nbytes * HASTE), transcendentals=0)


LIMITS = {"flows": 26, "pair_sum": 26, "overload": 26, "sens": 26, "add_last": 26}


def call(body, name, out_shape, in_specs, out_specs, scratch, estimate, aliases={}):
    return pl.pallas_call(
        body,
        out_shape=out_shape,
        in_specs=in_specs,
        out_specs=out_specs,
        scratch_shapes=scratch,
        input_output_aliases=aliases,
        compiler_params=pltpu.CompilerParams(vmem_limit_bytes=LIMITS[name] * MIB),
        cost_estimate=estimate,
        name=name,
    )


def resident(x):
    return pltpu.with_memory_space_constraint(x, pltpu.VMEM)


def at(index, size):
    return pl.ds(pl.multiple_of(index * size, size), size)


def penalty_and_adjoint(flows, limits):
    magnitude = jnp.sqrt(flows * flows + 1.0)
    zvalue = 4.0 * (magnitude / limits - 1.0)
    penalty = (jnp.maximum(zvalue, 0.0) + jnp.log1p(jnp.exp(-jnp.abs(zvalue)))) * 0.25
    adjoint = jax.nn.sigmoid(zvalue) * flows / (magnitude * limits)
    return penalty, adjoint


def flows_kernel(first, bounds, depth, block, pos, slab, codes, *refs):
    refs = list(refs)
    before = refs.pop(0) if bounds[0] > 0 else None
    held = refs.pop(0) if first else slab
    last = bounds[1] * depth == held.shape[1]
    outs = [refs.pop(0), refs.pop(0)] if last else []
    total = refs.pop(0)
    drawn, code_sem = refs.pop(0), refs.pop(0)
    slab_sem = refs.pop(0) if first else None
    out_sem = refs.pop(0) if last else None
    rows, hours = total.shape
    lo, hi = bounds

    def fetch(j):
        copies = [
            pltpu.make_async_copy(
                codes.at[at(j, depth), at(pos[block], hours)], drawn.at[j - lo], code_sem.at[j - lo]
            )
        ]
        if first:
            cols = at(j, depth)
            copies.append(pltpu.make_async_copy(slab.at[:, cols], held.at[:, cols], slab_sem.at[j]))
        return copies

    for j in range(lo, hi):
        for copy in fetch(j):
            copy.start()

    own = rows // 8
    stores = []

    def leave(chip):
        for side, core in ((0, pos[1]), (1, 1 - pos[1])):
            stores.append(
                pltpu.make_async_copy(
                    total.at[at(2 * chip + core, own), :],
                    outs[side].at[chip * own : (chip + 1) * own, :],
                    out_sem.at[2 * chip + side],
                )
            )
            stores[-1].start()

    def step(j, add, final=False):
        for copy in fetch(j):
            copy.wait()
        injections = (drawn[j - lo].astype(F32) * (1.0 / 1024.0)).astype(BF16)
        for chip in range(4):
            here = slice(2 * chip * own, 2 * (chip + 1) * own)
            part = jnp.dot(held[here, at(j, depth)], injections, preferred_element_type=F32)
            total[here, :] = part if add is None else add[here, :] + part
            if final:
                leave(chip)

    step(lo, before)

    @pl.loop(lo + 1, hi - last)
    def _(j):
        step(j, total)

    if last:
        step(hi - 1, total, True)
        for copy in stores:
            copy.wait()


def partial_flows(pos, slab, codes, block, hours, first=False, bounds=None, before=None):
    rows, buses = slab.shape
    depth = min(512, buses)
    steps = buses // depth
    bounds = bounds or (0, steps)
    last = bounds[1] == steps
    count = bounds[1] - bounds[0]
    out_shape, out_specs = [], []
    if first:
        out_shape, out_specs = [pltpu.VMEM(slab.shape, BF16)], [FAST]
    scratch = []
    if last:
        out_shape += [jax.ShapeDtypeStruct((rows // 2, hours), F32)] * 2
        out_specs += [HBM] * 2
        scratch.append(pltpu.VMEM((rows, hours), F32))
    else:
        out_shape.append(pltpu.VMEM((rows, hours), F32))
        out_specs.append(FAST)
    scratch += [pltpu.VMEM((count, depth, hours), jnp.int32), pltpu.SemaphoreType.DMA((count,))]
    if first:
        scratch.append(pltpu.SemaphoreType.DMA((count,)))
    else:
        slab = resident(slab)
    if last:
        scratch.append(pltpu.SemaphoreType.DMA((8,)))
    operands = [pos, slab, codes]
    in_specs = [WORDS, HBM if first else FAST, HBM]
    if before is not None:
        operands.append(resident(before))
        in_specs.append(FAST)
    return call(
        functools.partial(flows_kernel, first, bounds, depth, block),
        "flows",
        out_shape,
        in_specs,
        out_specs,
        scratch,
        cost(2 * rows * count * depth * hours, (2 * rows if first else 4 * hours) * count * depth),
    )(*operands)


def pair_kernel(pos, slab, keep, came, *refs):
    outs, (a, b, mine, sends, in_sem, out_sem) = refs[:4], refs[4:]
    own = mine.shape[0]
    copies, done = [], []
    for k in range(4):
        rows = at(lax.rem(pos[0] + k, 4), own)
        for n, (src, dst) in enumerate(((keep, a), (came, b))):
            copies.append(pltpu.make_async_copy(src.at[rows, :], dst.at[k], in_sem.at[2 * k + n]))
            copies[-1].start()
    for k in (1, 2, 3, 0):
        copies[2 * k].wait()
        copies[2 * k + 1].wait()
        both = a[k] + b[k]
        if k:
            sends[k - 1] = both.astype(BF16)
        else:
            mine[...] = both
        done.append(pltpu.make_async_copy(sends.at[k - 1] if k else mine, outs[k], out_sem.at[k]))
        done[-1].start()
    for copy in done:
        copy.wait()


def pair_sum(pos, slab, keep, came):
    rows, hours = keep.shape
    own = rows // 4
    shard = jax.ShapeDtypeStruct((own, hours), BF16)
    return call(
        pair_kernel,
        "pair_sum",
        [jax.ShapeDtypeStruct((own, hours), F32)] + [shard] * 3,
        [WORDS, FAST, HBM, HBM],
        [HBM] * 4,
        [
            pltpu.VMEM((4, own, hours), F32),
            pltpu.VMEM((4, own, hours), F32),
            pltpu.VMEM((own, hours), F32),
            pltpu.VMEM((3, own, hours), BF16),
            pltpu.SemaphoreType.DMA((8,)),
            pltpu.SemaphoreType.DMA((4,)),
        ],
        cost(rows * hours, 10 * rows * hours),
    )(pos, resident(slab), keep, came)


def overload_kernel(others, block, parts, part, pos, slab, codes, mine, *refs):
    came, refs = refs[:others], refs[others:]
    penalty, adjoint, held, got, drawn, pen, adj, in_sem, out_sem = refs[-9:]
    own, hours = mine.shape
    copies = [
        pltpu.make_async_copy(codes, drawn, in_sem.at[0]),
        pltpu.make_async_copy(mine, held, in_sem.at[1]),
    ]
    for n in range(others):
        copies.append(pltpu.make_async_copy(came[n], got.at[n], in_sem.at[2 + n]))
    for copy in copies:
        copy.start()
    for copy in copies:
        copy.wait()
    flows = held[...]
    for n in range(others):
        flows += got[n].astype(F32)
    lines = own // drawn.shape[1]
    first = (2 * pos[0] + pos[1]) * lines
    limits = jnp.concatenate([drawn[pl.ds(first + n, 1), :] for n in range(lines)], 1).astype(F32) / 64.0
    value, slope = penalty_and_adjoint(flows.T, limits)
    adj[...] = slope.astype(BF16)
    send = pltpu.make_async_copy(adj, adjoint, out_sem.at[0])
    send.start()
    pen[...] = value.T
    cols = at(pos[block] * parts + part, hours)
    store = pltpu.make_async_copy(pen, penalty.at[:, cols], out_sem.at[1])
    store.start()
    send.wait()
    store.wait()


def overload(pos, slab, codes, mine, came, penalty, hours_all, block, parts=1, part=0):
    own, hours = mine.shape
    operands = [pos, resident(slab), codes, mine, *came]
    aliases = {}
    if penalty is not None:
        aliases = {len(operands): 0}
        operands.append(penalty)
    return call(
        functools.partial(overload_kernel, len(came), block, parts, part),
        "overload",
        (jax.ShapeDtypeStruct((own, hours_all), F32), jax.ShapeDtypeStruct((hours, own), BF16)),
        [WORDS, FAST] + [HBM] * (len(operands) - 2),
        (HBM, HBM),
        [
            pltpu.VMEM((own, hours), F32),
            pltpu.VMEM((3, own, hours), BF16),
            pltpu.VMEM(codes.shape, jnp.int32),
            pltpu.VMEM((own, hours), F32),
            pltpu.VMEM((hours, own), BF16),
            pltpu.SemaphoreType.DMA((5,)),
            pltpu.SemaphoreType.DMA((2,)),
        ],
        cost(20 * mine.size, 16 * mine.size),
        aliases=aliases,
    )(*operands)


def sens_kernel(halves, block, adds, pos, slab, *refs):
    shards, refs = refs[:8], refs[8:]
    extra, refs = refs[:adds], refs[adds:]
    outs, (adjoint, got, made, shard_sem, got_sem, out_sem) = refs[: len(halves)], refs[len(halves) :]
    rows = adjoint.shape[1]
    own = rows // 8
    steps = made.shape[0] // len(halves)
    copies = []
    for k in range(8):
        slot = 2 * lax.rem(pos[0] + 4 - k % 4, 4) + (pos[1] if k < 4 else 1 - pos[1])
        copies.append(pltpu.make_async_copy(shards[k], adjoint.at[:, at(slot, own)], shard_sem.at[k]))
    arrivals = [pltpu.make_async_copy(extra[n], got.at[n], got_sem.at[n]) for n in range(adds)]
    for copy in copies + arrivals:
        copy.start()
    for copy in copies:
        copy.wait()

    def store(n, i):
        return pltpu.make_async_copy(made.at[n * steps + i], outs[n].at[:, at(i, block)], out_sem.at[n * steps + i])

    for n, half in enumerate(halves):
        if adds:
            arrivals[n].wait()

        @pl.loop(0, steps)
        def _(i):
            part = jnp.dot(adjoint[...], slab[:, at(half * steps + i, block)], preferred_element_type=F32)
            if adds:
                part += got[n, :, at(i, block)].astype(F32)
            made[n * steps + i] = part.astype(made.dtype)
            store(n, i).start()

    for n in range(len(halves)):
        for i in range(steps):
            store(n, i).wait()


def partial_sens(pos, slab, shards, halves, adds=(), dtype=BF16):
    rows, buses = slab.shape
    hours = shards[0].shape[0]
    block = min(1024, buses // 2)
    steps = buses // 2 // block * len(halves)
    return call(
        functools.partial(sens_kernel, halves, block, len(adds)),
        "sens",
        [jax.ShapeDtypeStruct((hours, buses // 2), dtype)] * len(halves),
        [WORDS, FAST] + [HBM] * (8 + len(adds)),
        [HBM] * len(halves),
        [
            pltpu.VMEM((hours, rows), BF16),
            pltpu.VMEM((len(adds), hours, buses // 2) if adds else (1, 16, 128), BF16),
            pltpu.VMEM((steps, hours, block), dtype),
            pltpu.SemaphoreType.DMA((8,)),
            pltpu.SemaphoreType.DMA((max(1, len(adds)),)),
            pltpu.SemaphoreType.DMA((steps,)),
        ],
        cost(rows * buses * hours * len(halves), buses * hours * len(halves)),
    )(pos, resident(slab), *shards, *adds)


def add_kernel(half, block, total, came, *refs):
    out, a, b, c, in_sem, out_sem = refs[-6:]
    steps = a.shape[0]

    def fetch(i):
        cols = at(i, block)
        return (
            pltpu.make_async_copy(total.at[:, cols], a.at[i], in_sem.at[0, i]),
            pltpu.make_async_copy(came.at[:, cols], b.at[i], in_sem.at[1, i]),
        )

    def store(i):
        return pltpu.make_async_copy(c.at[i], out.at[at(half * steps + i, block), :], out_sem.at[i])

    for i in range(steps):
        for copy in fetch(i):
            copy.start()

    @pl.loop(0, steps)
    def _(i):
        for copy in fetch(i):
            copy.wait()
        c[i] = (a[i] + b[i].astype(F32)).T
        store(i).start()

    for i in range(steps):
        store(i).wait()


def add_last(total, came, half, into):
    hours, buses = total.shape
    block = min(512, buses)
    steps = buses // block
    operands = [total, came] + ([] if into is None else [into])
    return call(
        functools.partial(add_kernel, half, block),
        "add_last",
        jax.ShapeDtypeStruct((2 * buses, hours), F32),
        [HBM] * len(operands),
        HBM,
        [
            pltpu.VMEM((steps, hours, block), F32),
            pltpu.VMEM((steps, hours, block), BF16),
            pltpu.VMEM((steps, block, hours), F32),
            pltpu.SemaphoreType.DMA((2, steps)),
            pltpu.SemaphoreType.DMA((steps,)),
        ],
        cost(came.size, 10 * came.size),
        aliases={} if into is None else {2: 0},
    )(*operands)


def local_tree(ptdf, load_codes, limit_codes):
    rows, buses = ptdf.shape
    hours_all = load_codes.shape[1]
    wide = hours_all // 4
    me, spot = lax.axis_index("br"), lax.axis_index("bus")
    pos = jnp.stack([spot // 2, spot % 2, me ^ 3, me ^ 1, me ^ 2, me]).astype(jnp.int32)
    limits = limit_codes.reshape(rows // 128, 128)
    far, over, up, home = 2, 3, 4, 5
    order = [pos]

    def run(kernel, *operands, **options):
        out = kernel(order[0], *operands, **options)
        order[0], _ = lax.optimization_barrier((order[0], jax.tree.leaves(out)[-1]))
        return out

    def across(x, bit):
        return lax.ppermute(x, "br", [(i, i ^ bit) for i in range(4)])

    def swap(x):
        return lax.ppermute(x, "bus", [(i, i ^ 1) for i in range(8)])

    def chip_ahead(x, k):
        return lax.ppermute(x, "bus", [(i, (i + 2 * k) % 8) for i in range(8)])

    def flows(block, **options):
        return run(partial_flows, slab, load_codes, block, wide, **options)

    def gate(x):
        return lax.optimization_barrier((x, order[0]))[0]

    def pair(keep, away):
        mine, *sends = run(pair_sum, slab, keep, swap(gate(away)))
        return mine, [chip_ahead(x, k + 1) for k, x in enumerate(sends)]

    penalty = None

    def adjoints(flow, block):
        nonlocal penalty
        mine, came = flow
        penalty, adjoint = run(overload, slab, limits, mine, came, penalty, hours_all, block)
        return [adjoint] + [chip_ahead(adjoint, k) for k in (1, 2, 3)]

    def shared(shards):
        return shards + [swap(gate(x)) for x in shards]

    def sens(shards, halves, **options):
        return run(partial_sens, slab, shards, halves, **options)

    def arrived(*xs):
        order[0], *_ = lax.optimization_barrier((order[0], *xs))

    slab = ptdf
    slab, keep, away = flows(far, first=True)
    flow_far = pair(keep, away)
    over_parts = flows(over)
    adj_far = adjoints(flow_far, far)
    flow_over = pair(*over_parts)
    up_parts = flows(up)
    far_a, far_b = sens(shared(adj_far), (0, 1))
    far_a, far_b = across(far_a, 1), across(far_b, 2)
    adj_over = adjoints(flow_over, over)
    flow_up = pair(*up_parts)
    home_parts = flows(home)
    adj_up = adjoints(flow_up, up)
    adj_over = shared(adj_over)
    over_a = across(sens(adj_over, (0,))[0], 1)
    flow_home = pair(*home_parts)
    adj_up = shared(adj_up)
    up_b = across(sens(adj_up, (1,))[0], 2)
    arrived(far_a, far_b)
    over_b = across(sens(adj_over, (1,), adds=(far_b,))[0], 1)
    up_a = across(sens(adj_up, (0,), adds=(far_a,))[0], 2)
    adj_home = adjoints(flow_home, home)
    total_a, total_b = sens(shared(adj_home), (0, 1), adds=(over_a, up_b), dtype=F32)
    total = add_last(total_b, over_b, 1, None)
    return penalty, add_last(total_a, up_a, 0, total)


def local_general(ptdf, load_codes, limit_codes):
    own = ptdf.shape[0] // lax.axis_size("bus")
    injections = (load_codes.astype(F32) / 1024.0).astype(BF16)
    flows = lax.psum_scatter(
        jnp.dot(ptdf, injections, preferred_element_type=F32), "bus", scatter_dimension=0, tiled=True
    )
    codes = lax.dynamic_slice_in_dim(limit_codes, lax.axis_index("bus") * own, own, 0)
    penalty, mine = penalty_and_adjoint(flows, codes.astype(F32)[:, None] / 64.0)
    adjoint = lax.all_gather(mine.astype(BF16), "bus", axis=0, tiled=True)
    part = lax.dot_general(ptdf, adjoint, (((0,), (0,)), ((), ())), preferred_element_type=F32)
    return penalty, lax.psum_scatter(part, "br", scatter_dimension=1, tiled=True)


def solution(mesh):
    tree = mesh.shape["br"] == 4 and mesh.shape["bus"] == 8
    return jax.shard_map(
        local_tree if tree else local_general,
        mesh=mesh,
        in_specs=(P("br", "bus"), P("bus", None), P("br")),
        out_specs=(P(("br", "bus"), None), P("bus", "br")),
        check_vma=False,
    )
```

```python
import functools

import jax
import jax.numpy as jnp
from jax import lax
from jax.experimental import pallas as pl
from jax.experimental.pallas import tpu as pltpu
from jax.sharding import PartitionSpec as P

MIB = 2**20
HASTE = 0.4
HBM = pl.BlockSpec(memory_space=pl.ANY)
FAST = pl.BlockSpec(memory_space=pltpu.VMEM)
WORDS = pl.BlockSpec(memory_space=pltpu.SMEM)
BF16, F32 = jnp.bfloat16, jnp.float32


def cost(flops, nbytes):
    return pl.CostEstimate(flops=int(flops * HASTE), bytes_accessed=int(nbytes * HASTE), transcendentals=0)


LIMITS = {"flows": 26, "pair_sum": 26, "overload": 26, "sens": 26, "add_last": 26}


def call(body, name, out_shape, in_specs, out_specs, scratch, estimate, aliases={}):
    return pl.pallas_call(
        body,
        out_shape=out_shape,
        in_specs=in_specs,
        out_specs=out_specs,
        scratch_shapes=scratch,
        input_output_aliases=aliases,
        compiler_params=pltpu.CompilerParams(vmem_limit_bytes=LIMITS[name] * MIB),
        cost_estimate=estimate,
        name=name,
    )


def resident(x):
    return pltpu.with_memory_space_constraint(x, pltpu.VMEM)


def at(index, size):
    return pl.ds(pl.multiple_of(index * size, size), size)


def penalty_and_adjoint(flows, limits):
    magnitude = jnp.sqrt(flows * flows + 1.0)
    zvalue = 4.0 * (magnitude / limits - 1.0)
    penalty = (jnp.maximum(zvalue, 0.0) + jnp.log1p(jnp.exp(-jnp.abs(zvalue)))) * 0.25
    adjoint = jax.nn.sigmoid(zvalue) * flows / (magnitude * limits)
    return penalty, adjoint


def flows_kernel(first, bounds, depth, block, pos, slab, codes, *refs):
    refs = list(refs)
    before = refs.pop(0) if bounds[0] > 0 else None
    held = refs.pop(0) if first else slab
    last = bounds[1] * depth == held.shape[1]
    outs = [refs.pop(0), refs.pop(0)] if last else []
    total = refs.pop(0)
    drawn, code_sem = refs.pop(0), refs.pop(0)
    slab_sem = refs.pop(0) if first else None
    out_sem = refs.pop(0) if last else None
    rows, hours = total.shape
    lo, hi = bounds

    def fetch(j):
        copies = [
            pltpu.make_async_copy(
                codes.at[at(j, depth), at(pos[block], hours)], drawn.at[j - lo], code_sem.at[j - lo]
            )
        ]
        if first:
            cols = at(j, depth)
            copies.append(pltpu.make_async_copy(slab.at[:, cols], held.at[:, cols], slab_sem.at[j]))
        return copies

    for j in range(lo, hi):
        for copy in fetch(j):
            copy.start()

    own = rows // 8
    stores = []

    def leave(chip):
        for side, core in ((0, pos[1]), (1, 1 - pos[1])):
            stores.append(
                pltpu.make_async_copy(
                    total.at[at(2 * chip + core, own), :],
                    outs[side].at[chip * own : (chip + 1) * own, :],
                    out_sem.at[2 * chip + side],
                )
            )
            stores[-1].start()

    def step(j, add, final=False):
        for copy in fetch(j):
            copy.wait()
        injections = (drawn[j - lo].astype(F32) * (1.0 / 1024.0)).astype(BF16)
        for chip in range(4):
            here = slice(2 * chip * own, 2 * (chip + 1) * own)
            part = jnp.dot(held[here, at(j, depth)], injections, preferred_element_type=F32)
            total[here, :] = part if add is None else add[here, :] + part
            if final:
                leave(chip)

    step(lo, before)

    @pl.loop(lo + 1, hi - last)
    def _(j):
        step(j, total)

    if last:
        step(hi - 1, total, True)
        for copy in stores:
            copy.wait()


def partial_flows(pos, slab, codes, block, hours, first=False, bounds=None, before=None):
    rows, buses = slab.shape
    depth = min(512, buses)
    steps = buses // depth
    bounds = bounds or (0, steps)
    last = bounds[1] == steps
    count = bounds[1] - bounds[0]
    out_shape, out_specs = [], []
    if first:
        out_shape, out_specs = [pltpu.VMEM(slab.shape, BF16)], [FAST]
    scratch = []
    if last:
        out_shape += [jax.ShapeDtypeStruct((rows // 2, hours), F32)] * 2
        out_specs += [HBM] * 2
        scratch.append(pltpu.VMEM((rows, hours), F32))
    else:
        out_shape.append(pltpu.VMEM((rows, hours), F32))
        out_specs.append(FAST)
    scratch += [pltpu.VMEM((count, depth, hours), jnp.int32), pltpu.SemaphoreType.DMA((count,))]
    if first:
        scratch.append(pltpu.SemaphoreType.DMA((count,)))
    else:
        slab = resident(slab)
    if last:
        scratch.append(pltpu.SemaphoreType.DMA((8,)))
    operands = [pos, slab, codes]
    in_specs = [WORDS, HBM if first else FAST, HBM]
    if before is not None:
        operands.append(resident(before))
        in_specs.append(FAST)
    return call(
        functools.partial(flows_kernel, first, bounds, depth, block),
        "flows",
        out_shape,
        in_specs,
        out_specs,
        scratch,
        cost(2 * rows * count * depth * hours, (2 * rows if first else 4 * hours) * count * depth),
    )(*operands)


def pair_kernel(pos, slab, keep, came, *refs):
    outs, (a, b, mine, sends, in_sem, out_sem) = refs[:4], refs[4:]
    own = mine.shape[0]
    copies, done = [], []
    for k in range(4):
        rows = at(lax.rem(pos[0] + k, 4), own)
        for n, (src, dst) in enumerate(((keep, a), (came, b))):
            copies.append(pltpu.make_async_copy(src.at[rows, :], dst.at[k], in_sem.at[2 * k + n]))
            copies[-1].start()
    for k in (1, 2, 3, 0):
        copies[2 * k].wait()
        copies[2 * k + 1].wait()
        both = a[k] + b[k]
        if k:
            sends[k - 1] = both.astype(BF16)
        else:
            mine[...] = both
        done.append(pltpu.make_async_copy(sends.at[k - 1] if k else mine, outs[k], out_sem.at[k]))
        done[-1].start()
    for copy in done:
        copy.wait()


def pair_sum(pos, slab, keep, came):
    rows, hours = keep.shape
    own = rows // 4
    shard = jax.ShapeDtypeStruct((own, hours), BF16)
    return call(
        pair_kernel,
        "pair_sum",
        [jax.ShapeDtypeStruct((own, hours), F32)] + [shard] * 3,
        [WORDS, FAST, HBM, HBM],
        [HBM] * 4,
        [
            pltpu.VMEM((4, own, hours), F32),
            pltpu.VMEM((4, own, hours), F32),
            pltpu.VMEM((own, hours), F32),
            pltpu.VMEM((3, own, hours), BF16),
            pltpu.SemaphoreType.DMA((8,)),
            pltpu.SemaphoreType.DMA((4,)),
        ],
        cost(rows * hours, 10 * rows * hours),
    )(pos, resident(slab), keep, came)


def overload_kernel(others, block, parts, part, pos, slab, codes, mine, *refs):
    came, refs = refs[:others], refs[others:]
    penalty, adjoint, held, got, drawn, pen, adj, in_sem, out_sem = refs[-9:]
    own, hours = mine.shape
    copies = [
        pltpu.make_async_copy(codes, drawn, in_sem.at[0]),
        pltpu.make_async_copy(mine, held, in_sem.at[1]),
    ]
    for n in range(others):
        copies.append(pltpu.make_async_copy(came[n], got.at[n], in_sem.at[2 + n]))
    for copy in copies:
        copy.start()
    for copy in copies:
        copy.wait()
    flows = held[...]
    for n in range(others):
        flows += got[n].astype(F32)
    lines = own // drawn.shape[1]
    first = (2 * pos[0] + pos[1]) * lines
    limits = jnp.concatenate([drawn[pl.ds(first + n, 1), :] for n in range(lines)], 1).astype(F32) / 64.0
    value, slope = penalty_and_adjoint(flows.T, limits)
    adj[...] = slope.astype(BF16)
    send = pltpu.make_async_copy(adj, adjoint, out_sem.at[0])
    send.start()
    pen[...] = value.T
    cols = at(pos[block] * parts + part, hours)
    store = pltpu.make_async_copy(pen, penalty.at[:, cols], out_sem.at[1])
    store.start()
    send.wait()
    store.wait()


def overload(pos, slab, codes, mine, came, penalty, hours_all, block, parts=1, part=0):
    own, hours = mine.shape
    operands = [pos, resident(slab), codes, mine, *came]
    aliases = {}
    if penalty is not None:
        aliases = {len(operands): 0}
        operands.append(penalty)
    return call(
        functools.partial(overload_kernel, len(came), block, parts, part),
        "overload",
        (jax.ShapeDtypeStruct((own, hours_all), F32), jax.ShapeDtypeStruct((hours, own), BF16)),
        [WORDS, FAST] + [HBM] * (len(operands) - 2),
        (HBM, HBM),
        [
            pltpu.VMEM((own, hours), F32),
            pltpu.VMEM((3, own, hours), BF16),
            pltpu.VMEM(codes.shape, jnp.int32),
            pltpu.VMEM((own, hours), F32),
            pltpu.VMEM((hours, own), BF16),
            pltpu.SemaphoreType.DMA((5,)),
            pltpu.SemaphoreType.DMA((2,)),
        ],
        cost(20 * mine.size, 16 * mine.size),
        aliases=aliases,
    )(*operands)


def sens_kernel(halves, block, adds, pos, slab, *refs):
    shards, refs = refs[:8], refs[8:]
    extra, refs = refs[:adds], refs[adds:]
    outs, (adjoint, got, made, shard_sem, got_sem, out_sem) = refs[: len(halves)], refs[len(halves) :]
    rows = adjoint.shape[1]
    own = rows // 8
    steps = made.shape[0] // len(halves)
    copies = []
    for k in range(8):
        slot = 2 * lax.rem(pos[0] + 4 - k % 4, 4) + (pos[1] if k < 4 else 1 - pos[1])
        copies.append(pltpu.make_async_copy(shards[k], adjoint.at[:, at(slot, own)], shard_sem.at[k]))
    arrivals = [pltpu.make_async_copy(extra[n], got.at[n], got_sem.at[n]) for n in range(adds)]
    for copy in copies + arrivals:
        copy.start()
    for copy in copies:
        copy.wait()

    def store(n, i):
        return pltpu.make_async_copy(made.at[n * steps + i], outs[n].at[:, at(i, block)], out_sem.at[n * steps + i])

    for n, half in enumerate(halves):
        if adds:
            arrivals[n].wait()

        @pl.loop(0, steps)
        def _(i):
            part = jnp.dot(adjoint[...], slab[:, at(half * steps + i, block)], preferred_element_type=F32)
            if adds:
                part += got[n, :, at(i, block)].astype(F32)
            made[n * steps + i] = part.astype(made.dtype)
            store(n, i).start()

    for n in range(len(halves)):
        for i in range(steps):
            store(n, i).wait()


def partial_sens(pos, slab, shards, halves, adds=(), dtype=BF16):
    rows, buses = slab.shape
    hours = shards[0].shape[0]
    block = min(1024, buses // 2)
    steps = buses // 2 // block * len(halves)
    return call(
        functools.partial(sens_kernel, halves, block, len(adds)),
        "sens",
        [jax.ShapeDtypeStruct((hours, buses // 2), dtype)] * len(halves),
        [WORDS, FAST] + [HBM] * (8 + len(adds)),
        [HBM] * len(halves),
        [
            pltpu.VMEM((hours, rows), BF16),
            pltpu.VMEM((len(adds), hours, buses // 2) if adds else (1, 16, 128), BF16),
            pltpu.VMEM((steps, hours, block), dtype),
            pltpu.SemaphoreType.DMA((8,)),
            pltpu.SemaphoreType.DMA((max(1, len(adds)),)),
            pltpu.SemaphoreType.DMA((steps,)),
        ],
        cost(rows * buses * hours * len(halves), buses * hours * len(halves)),
    )(pos, resident(slab), *shards, *adds)


def add_kernel(half, block, total, came, *refs):
    out, a, b, c, in_sem, out_sem = refs[-6:]
    steps = a.shape[0]

    def fetch(i):
        cols = at(i, block)
        return (
            pltpu.make_async_copy(total.at[:, cols], a.at[i], in_sem.at[0, i]),
            pltpu.make_async_copy(came.at[:, cols], b.at[i], in_sem.at[1, i]),
        )

    def store(i):
        return pltpu.make_async_copy(c.at[i], out.at[at(half * steps + i, block), :], out_sem.at[i])

    for i in range(steps):
        for copy in fetch(i):
            copy.start()

    @pl.loop(0, steps)
    def _(i):
        for copy in fetch(i):
            copy.wait()
        c[i] = (a[i] + b[i].astype(F32)).T
        store(i).start()

    for i in range(steps):
        store(i).wait()


def add_last(total, came, half, into):
    hours, buses = total.shape
    block = min(512, buses)
    steps = buses // block
    operands = [total, came] + ([] if into is None else [into])
    return call(
        functools.partial(add_kernel, half, block),
        "add_last",
        jax.ShapeDtypeStruct((2 * buses, hours), F32),
        [HBM] * len(operands),
        HBM,
        [
            pltpu.VMEM((steps, hours, block), F32),
            pltpu.VMEM((steps, hours, block), BF16),
            pltpu.VMEM((steps, block, hours), F32),
            pltpu.SemaphoreType.DMA((2, steps)),
            pltpu.SemaphoreType.DMA((steps,)),
        ],
        cost(came.size, 10 * came.size),
        aliases={} if into is None else {2: 0},
    )(*operands)


def local_tree(ptdf, load_codes, limit_codes):
    rows, buses = ptdf.shape
    hours_all = load_codes.shape[1]
    wide = hours_all // 4
    me, spot = lax.axis_index("br"), lax.axis_index("bus")
    pos = jnp.stack([spot // 2, spot % 2, me ^ 3, me ^ 1, me ^ 2, me]).astype(jnp.int32)
    limits = limit_codes.reshape(rows // 128, 128)
    far, over, up, home = 2, 3, 4, 5
    order = [pos]

    def run(kernel, *operands, **options):
        out = kernel(order[0], *operands, **options)
        order[0], _ = lax.optimization_barrier((order[0], jax.tree.leaves(out)[-1]))
        return out

    def across(x, bit):
        return lax.ppermute(x, "br", [(i, i ^ bit) for i in range(4)])

    def swap(x):
        return lax.ppermute(x, "bus", [(i, i ^ 1) for i in range(8)])

    def chip_ahead(x, k):
        return lax.ppermute(x, "bus", [(i, (i + 2 * k) % 8) for i in range(8)])

    def flows(block, **options):
        return run(partial_flows, slab, load_codes, block, wide, **options)

    def gate(x):
        return lax.optimization_barrier((x, order[0]))[0]

    def pair(keep, away):
        mine, *sends = run(pair_sum, slab, keep, swap(gate(away)))
        return mine, [chip_ahead(x, k + 1) for k, x in enumerate(sends)]

    penalty = None

    def adjoints(flow, block):
        nonlocal penalty
        mine, came = flow
        penalty, adjoint = run(overload, slab, limits, mine, came, penalty, hours_all, block)
        return [adjoint] + [chip_ahead(adjoint, k) for k in (1, 2, 3)]

    def shared(shards):
        return shards + [swap(gate(x)) for x in shards]

    def sens(shards, halves, **options):
        return run(partial_sens, slab, shards, halves, **options)

    def arrived(*xs):
        order[0], *_ = lax.optimization_barrier((order[0], *xs))

    slab = ptdf
    slab, keep, away = flows(far, first=True)
    flow_far = pair(keep, away)
    over_parts = flows(over)
    adj_far = adjoints(flow_far, far)
    flow_over = pair(*over_parts)
    up_parts = flows(up)
    adj_far = shared(adj_far)
    arrived(*flow_over[1])
    far_a, far_b = sens(adj_far, (0, 1))
    far_a, far_b = across(far_a, 1), across(far_b, 2)
    adj_over = adjoints(flow_over, over)
    flow_up = pair(*up_parts)
    home_parts = flows(home)
    arrived(*adj_over)
    adj_up = adjoints(flow_up, up)
    adj_over = shared(adj_over)
    (over_a,) = sens(adj_over, (0,))
    adj_up = shared(adj_up)
    arrived(far_a, far_b)
    (up_b,) = sens(adj_up, (1,))
    over_a, up_b = across(gate(over_a), 1), across(up_b, 2)
    flow_home = pair(*home_parts)
    over_b = across(sens(adj_over, (1,), adds=(far_b,))[0], 1)
    up_a = across(sens(adj_up, (0,), adds=(far_a,))[0], 2)
    arrived(over_a, up_b)
    adj_home = adjoints(flow_home, home)
    total_a, total_b = sens(shared(adj_home), (0, 1), adds=(over_a, up_b), dtype=F32)
    total = add_last(total_b, over_b, 1, None)
    return penalty, add_last(total_a, up_a, 0, total)


def local_general(ptdf, load_codes, limit_codes):
    own = ptdf.shape[0] // lax.axis_size("bus")
    injections = (load_codes.astype(F32) / 1024.0).astype(BF16)
    flows = lax.psum_scatter(
        jnp.dot(ptdf, injections, preferred_element_type=F32), "bus", scatter_dimension=0, tiled=True
    )
    codes = lax.dynamic_slice_in_dim(limit_codes, lax.axis_index("bus") * own, own, 0)
    penalty, mine = penalty_and_adjoint(flows, codes.astype(F32)[:, None] / 64.0)
    adjoint = lax.all_gather(mine.astype(BF16), "bus", axis=0, tiled=True)
    part = lax.dot_general(ptdf, adjoint, (((0,), (0,)), ((), ())), preferred_element_type=F32)
    return penalty, lax.psum_scatter(part, "br", scatter_dimension=1, tiled=True)


def solution(mesh):
    tree = mesh.shape["br"] == 4 and mesh.shape["bus"] == 8
    return jax.shard_map(
        local_tree if tree else local_general,
        mesh=mesh,
        in_specs=(P("br", "bus"), P("bus", None), P("br")),
        out_specs=(P(("br", "bus"), None), P("bus", "br")),
        check_vma=False,
    )
```
